32 devices in a mesh: worker: 4 (over x, core), fsdp: 8 (over z, y).
Axes of the slice: x: 2, y: 2, z: 4, core: 2. Of those that a mesh axis runs over, the one named last changes fastest.
Arguments:
- inputs: bfloat16 [4, 2048, 8192], P('worker', 'fsdp'), may hold values from -6 to 6
- output_grads: bfloat16 [4, 2048, 1024], P('worker', 'fsdp'), may hold values from -0.3125 to 0.3125
- local_params: float32 [4, 8192, 1024], P('worker', 'fsdp'), may hold values from -6 to 6
- first_moment: float32 [4, 8192, 1024], P('worker', 'fsdp'), may hold values from -4 to 4
- second_moment: float32 [4, 8192, 1024], P('worker', 'fsdp'), may hold values from 0.01 to 0.1
- global_params: float32 [8192, 1024], P(('fsdp', 'worker')), may hold values from -6 to 6
- momentum: float32 [8192, 1024], P(('fsdp', 'worker')), may hold values from -6 to 6
Outputs:
- new_params: float32 [8192, 1024], P('fsdp')
- new_momentum: float32 [8192, 1024], P(('fsdp', 'worker'))
The draws below stay inside these ranges and needn't reach their ends.
All inputs are finite; a program needn't handle non-finite values.
Results may differ from the reference program's by a relative error of at most 0.0015.
Values may be sent and summed in bfloat16 or wider, within the bound.
No kernel may reach another device: no remote copies, remote signals or barrier semaphores. Data moves between devices by JAX's collectives and lax.ppermute only.
A program may use at most 128 MiB of HBM per device.

```python
import math
import jax
import jax.numpy as jnp
from jax import lax

D = 8192
KV = 1024
TOK_DEV = 256
TOKENS = 2048
N_WORKER = 4
N_FSDP = 8


def spiked(array, key, source, target, shards_of, factor):
    def block_of(dim):
        return (jnp.arange(array.shape[dim]) // (array.shape[dim] // shards_of)).reshape((-1,) + (1,) * (array.ndim - 1 - dim))

    one_side = jax.random.permutation(key, shards_of)[block_of(target)]
    second = (block_of(target) + shards_of // 2) % shards_of
    return jnp.where((block_of(source) == one_side) | (block_of(source) == second), factor * array, array)


def steps_of(own_key, extent, pieces, smallest, top_value):
    level, own = 1.0, jax.random.fold_in(own_key, 6)
    for axis_at, parts in pieces:
        draws = jnp.exp(jax.random.uniform(jax.random.fold_in(own, axis_at), (parts,), jnp.float32, smallest / len(pieces), top_value / len(pieces)))
        level = level * jnp.repeat(draws, extent[axis_at] // parts).reshape([-1 if axis == axis_at else 1 for axis in range(len(extent))])
    return level


def noise(stream_key, shape, width, reach, split=(), held_as=jnp.bfloat16):
    factor_of = steps_of(stream_key, shape, split, -0.22, 0.18) if split else 1.0
    entries = jax.random.normal(stream_key, shape, jnp.float32) * width * factor_of
    return jnp.minimum(jnp.maximum(entries, -reach), reach).astype(held_as)


def gaussian_with(rng, dims, width, bound, split, heavy, dtype=jnp.bfloat16):
    entries = width * jax.random.normal(rng, dims, jnp.float32)
    if split:
        entries = entries * steps_of(rng, dims, split, -0.22, 0.18)
    return jnp.clip(spiked(entries, jax.random.fold_in(rng, 3), *heavy), -bound, bound).astype(dtype)


def setup_inputs(seed: int = 0) -> dict:
    splits = jax.random.split(jax.random.key(seed), 8)
    inputs = gaussian_with(splits[0], (N_WORKER, TOKENS, D), 1.0, 6.0, ((0, 4), (1, 8)), (1, 2, 8, 2.0))
    output_grads = noise(splits[1], (N_WORKER, TOKENS, KV), (TOKENS ** -0.5), 0.3125, ((0, 4), (1, 8)))
    local_params = noise(splits[2], (N_WORKER, D, KV), 1.0, 6.0, ((0, 4), (1, 8)), jnp.float32)
    first_moment = noise(splits[3], (N_WORKER, D, KV), 0.3, 4.0, ((0, 4), (1, 8)), jnp.float32)
    second_moment = jnp.clip(jnp.exp(math.log(0.1) - 2.3025851 * jax.random.uniform(splits[4], (N_WORKER, D, KV), jnp.float32) ** steps_of(splits[4], (N_WORKER, D, KV), ((0, 4), (1, 8)), -0.2, 0.2)), 0.01, 0.1)
    global_params = noise(splits[5], (D, KV), 1.0, 6.0, ((0, 32),), jnp.float32)
    momentum = noise(splits[6], (D, KV), 0.5, 6.0, ((0, 32),), jnp.float32)
    return dict(inputs=inputs, output_grads=output_grads, local_params=local_params, first_moment=first_moment, second_moment=second_moment, global_params=global_params, momentum=momentum)


beta_first = 0.8
beta_second = 0.9
inner_rate = 0.15
weight_decay = 0.1
adam_epsilon = 1e-08
outer_rate = 0.7
momentum_coef = 0.9
inner_count = 50

def replica_gradient(operands):
    features, cotangents = operands

    def accumulate(source, total):
        begin_row = (source * TOK_DEV).astype(jnp.int32)
        block_in = lax.dynamic_slice_in_dim(features, begin_row, TOK_DEV, 0)
        block_out = lax.dynamic_slice_in_dim(cotangents, begin_row, TOK_DEV, 0)
        partial_term = lax.dot_general(block_in, block_out, (((0,), (0,)), ((), ())), preferred_element_type=jnp.float32)
        rounded = lax.optimization_barrier(partial_term.astype(jnp.bfloat16))
        return total + rounded.astype(jnp.float32)
    start_total = jnp.zeros((D, KV), jnp.float32)
    return lax.fori_loop(0, N_FSDP, accumulate, start_total)

def reference(inputs, output_grads, local_params, first_moment, second_moment, global_params, momentum):
    gradient = lax.map(replica_gradient, (inputs, output_grads))
    moment_one = beta_first * first_moment + (1.0 - beta_first) * gradient
    moment_two = beta_second * second_moment + (1.0 - beta_second) * gradient * gradient
    first_correction = 1.0 - beta_first ** inner_count
    second_correction = 1.0 - beta_second ** inner_count
    ratio = moment_one / first_correction / (jnp.sqrt(moment_two / second_correction) + adam_epsilon)
    stepped = local_params - inner_rate * (ratio + weight_decay * local_params)
    outer_grad = lax.optimization_barrier(jnp.sum(global_params[None] - stepped, axis=0)) / N_WORKER
    new_momentum = momentum_coef * momentum + outer_grad
    new_params = global_params - outer_rate * (outer_grad + momentum_coef * new_momentum)
    return (new_params, new_momentum)
```

```python
import functools
import math

import jax
import jax.numpy as jnp
from jax import lax
from jax.experimental import pallas as pl
from jax.experimental.pallas import tpu as pltpu
from jax.sharding import PartitionSpec as P

beta_first = 0.8
beta_second = 0.9
inner_rate = 0.15
weight_decay = 0.1
adam_epsilon = 1e-08
outer_rate = 0.7
momentum_coef = 0.9
inner_count = 50

TILE = 128
VMEM = 40 * 1024 * 1024


def chunks_of(rows):
    unit = 2 * TILE
    units = rows // unit
    sizes = [units - 1, 1] if units > 1 else [1]
    result, at = [], 0
    for size in sizes:
        result.append((at, size * unit))
        at += size * unit
    return result


def pairs(n, k, keep=lambda i: True):
    return [(i, i ^ k) for i in range(n) if keep(i)]


WINDOW = 5
COST = 4
PINNED = 2


class Mover:
    def __init__(self):
        self.done = []

    def __call__(self, v, axis, pairing):
        if len(self.done) >= WINDOW:
            v, _ = lax.optimization_barrier((v, self.done[-WINDOW]))
        arrived = lax.ppermute(v, axis, pairing)
        self.done.append(arrived)
        return arrived


def split_kernel(n, rows, pieces, info, x, *refs):
    outs, (buf, sem_in, sem_out) = refs[:-3], refs[-3:]
    reads, writes = [], []
    for k in range(n):
        start = pl.multiple_of((info[0] ^ k) * rows, TILE)
        reads.append(
            pltpu.make_async_copy(x.at[:, pl.ds(start, rows)], buf.at[k], sem_in.at[k])
        )
        reads[-1].start()
    for k in range(n):
        reads[k].wait()
        for j, (of, at, size) in enumerate(pieces):
            if of == k:
                copy = pltpu.make_async_copy(buf.at[k, :, pl.ds(at, size)], outs[j], sem_out.at[j])
                copy.start()
                writes.append(copy)
    for copy in writes:
        copy.wait()


def split_columns(info, x, n, rows, chunks):
    far = n // 2
    pieces = [(k, 0, rows) for k in range(far)]
    pieces += [(k, at, size) for at, size in chunks for k in range(far, n)]
    shapes = [jax.ShapeDtypeStruct((x.shape[0], size), x.dtype) for _, _, size in pieces]
    flat = pl.pallas_call(
        functools.partial(split_kernel, n, rows, pieces),
        in_specs=[pl.BlockSpec(memory_space=pltpu.SMEM), pl.BlockSpec(memory_space=pltpu.HBM)],
        out_specs=[pl.BlockSpec(memory_space=pltpu.HBM)] * len(shapes),
        scratch_shapes=[
            pltpu.VMEM((n, x.shape[0], rows), x.dtype),
            pltpu.SemaphoreType.DMA((n,)),
            pltpu.SemaphoreType.DMA((len(pieces),)),
        ],
        out_shape=shapes,
        compiler_params=pltpu.CompilerParams(vmem_limit_bytes=VMEM),
        name="split_columns",
    )(info, x)
    return flat[:far], [flat[far * (c + 1) : far * (c + 2)] for c in range(len(chunks))]


def exchange(move, block, whole, parts):
    n = lax.axis_size("fsdp")
    across = n // 4
    near, far = across, 2 * across
    gs = {0: block}
    xs = [{k: whole[k] for k in range(far)} for _ in parts]
    straight = [far, far + near]
    crossing = straight + [k for k in range(far, n) if k not in straight]

    def go(v, k):
        return move(v, "fsdp", pairs(n, k))

    def inside(*ks):
        for k in ks:
            arrived = go(whole[k], k)
            for x in xs:
                x[k] = arrived

    def cross(c, ks):
        for k in ks:
            xs[c][k] = go(parts[c][k - far], k)

    def spread(j):
        for k in range(1, across):
            gs[j + k] = go(gs[j], k)

    gs[far] = go(block, far)
    spread(0)
    inside(*range(1, across))
    gs[near] = go(block, near)
    cross(0, crossing[:1])
    gs[near + far] = go(gs[far], near)
    spread(far)
    cross(0, crossing[1:2])
    spread(near)
    inside(*range(near + 1, far))
    spread(near + far)
    cross(0, crossing[2:3])
    inside(near)
    cross(0, crossing[3:])
    for c in range(1, len(parts)):
        cross(c, crossing)
    return [gs[k] for k in range(n)], [[x[k] for k in range(n)] for x in xs], crossing


def step_kernel(n, half_tiles, at, share, scale, info, *refs):
    xs, gs = refs[:n], refs[n : 2 * n]
    params, first, second, anchor, momentum, send, keep = refs[2 * n :]
    gradient = None
    for x, g in zip(xs, gs):
        term = lax.dot_general(
            x[...], g[...], (((0,), (0,)), ((), ())), preferred_element_type=jnp.float32
        )
        gradient = term if gradient is None else gradient + term
    moment_one = beta_first * first[...] + (1.0 - beta_first) * gradient
    moment_two = beta_second * second[...] + (1.0 - beta_second) * gradient * gradient
    first_correction = 1.0 - beta_first**inner_count
    second_correction = 1.0 - beta_second**inner_count
    ratio = (
        moment_one
        * (1.0 / first_correction)
        / (jnp.sqrt(moment_two * (1.0 / second_correction)) + adam_epsilon)
    )
    stepped = params[...] - inner_rate * (ratio + weight_decay * params[...])
    i = pl.program_id(0)
    piece = min(share, TILE)
    offset = info[2] * share - (at + step_tile(i, info, half_tiles) * TILE)
    inside = (offset > -share) & (offset < TILE)

    def store(out):
        out[...] = stepped

        @pl.when(inside)
        def _():
            rows = pl.ds(pl.multiple_of(jnp.maximum(offset, 0), piece), piece)
            out[rows] += owner_term(anchor[...], momentum[...], scale)

    pl.when(i < half_tiles)(lambda: store(send))
    pl.when(i >= half_tiles)(lambda: store(keep))


def owner_term(anchor, momentum, scale):
    step = outer_rate * (1.0 + momentum_coef)
    return (scale * (1.0 - step) / step) * anchor - (
        scale * outer_rate * momentum_coef**2 / step
    ) * momentum


def step_tile(i, info, half_tiles):
    core = info[1]
    return jnp.where(i < half_tiles, (1 - core) * half_tiles + i, core * half_tiles + i - half_tiles)


def inner_step(info, xs, gs, params, first, second, anchor, momentum, scale, at, size):
    n = len(gs)
    tokens, width = gs[0].shape
    share = anchor.shape[0]
    half_tiles = size // TILE // 2
    piece = min(share, TILE)

    def tile(i, info):
        return step_tile(i, info, half_tiles)

    def owned(i, info):
        ahead = at + tile(i, info) * TILE - info[2] * share
        return (jnp.clip(ahead // piece, 0, share // piece - 1), 0)

    columns = [
        pl.BlockSpec(
            (tokens, TILE),
            lambda i, info, skip=0 if x.shape[1] == size else at // TILE: (0, skip + tile(i, info)),
        )
        for x in xs
    ]
    whole = pl.BlockSpec((tokens, width), lambda i, info: (0, 0))
    state = pl.BlockSpec((None, TILE, width), lambda i, info: (0, at // TILE + tile(i, info), 0))
    shape = jax.ShapeDtypeStruct((size // 2, width), jnp.float32)
    return pl.pallas_call(
        functools.partial(step_kernel, n, half_tiles, at, share, scale),
        grid_spec=pltpu.PrefetchScalarGridSpec(
            num_scalar_prefetch=1,
            grid=(2 * half_tiles,),
            in_specs=columns
            + [whole] * n
            + [state] * 3
            + [pl.BlockSpec((piece, width), owned)] * 2,
            out_specs=[
                pl.BlockSpec((TILE, width), lambda i, info: (jnp.minimum(i, half_tiles - 1), 0)),
                pl.BlockSpec((TILE, width), lambda i, info: (jnp.maximum(i - half_tiles, 0), 0)),
            ],
        ),
        out_shape=[shape, shape],
        compiler_params=pltpu.CompilerParams(vmem_limit_bytes=VMEM),
        cost_estimate=pl.CostEstimate(
            flops=COST * 2 * n * tokens * size * width,
            bytes_accessed=COST * 4 * size * width * 5,
            transcendentals=COST * size * width,
        ),
        name="inner_step",
    )(info, *xs, *gs, params, first, second, anchor, momentum)


def outer_kernel(at, half, share, info, mine, other, anchor, momentum, *refs):
    whole, fresh, buf, sem = refs[-4:]
    core, worker = info[1], info[2]
    copies = []
    for j, (source, side) in enumerate(((mine, core), (other, 1 - core))):
        rows = pl.ds(pl.multiple_of(at + side * half, TILE), half)
        copies.append(pltpu.make_async_copy(source, whole.at[rows], sem.at[j]))
        copies[-1].start()
    first = worker * share - at
    step = outer_rate * (1.0 + momentum_coef)

    @pl.when((first >= 0) & (first < 2 * half))
    def _():
        piece = math.gcd(share, half)
        for p in range(share // piece):
            row = first + p * piece
            side = row // half
            rows = pl.ds(pl.multiple_of(row - side * half, piece), piece)
            part = pl.ds(p * piece, piece)

            def momentum_of(source):
                buf[part] = (
                    (momentum_coef - outer_rate * momentum_coef**2 / step) * momentum[part]
                    + (1.0 + (1.0 - step) / step) * anchor[part]
                    - (1.0 / step) * source[rows]
                )

            pl.when(side == core)(lambda: momentum_of(mine))
            pl.when(side != core)(lambda: momentum_of(other))
        copy = pltpu.make_async_copy(buf, fresh, sem.at[2])
        copy.start()
        copy.wait()

    for copy in copies:
        copy.wait()


def outer_step(info, mine, other, anchor, momentum, state, rows, at):
    half, width = mine.shape
    share = anchor.shape[0]
    shapes = [
        jax.ShapeDtypeStruct((rows, width), jnp.float32),
        jax.ShapeDtypeStruct((share, width), jnp.float32),
    ]
    return pl.pallas_call(
        functools.partial(outer_kernel, at, half, share),
        in_specs=[pl.BlockSpec(memory_space=pltpu.SMEM)]
        + [pl.BlockSpec(memory_space=pltpu.VMEM)] * 4
        + [pl.BlockSpec(memory_space=pl.ANY)] * len(state),
        out_specs=[pl.BlockSpec(memory_space=pl.ANY)] * 2,
        out_shape=shapes,
        scratch_shapes=[
            pltpu.VMEM((share, width), jnp.float32),
            pltpu.SemaphoreType.DMA((3,)),
        ],
        input_output_aliases={5: 0, 6: 1} if state else {},
        compiler_params=pltpu.CompilerParams(vmem_limit_bytes=VMEM),
        name="outer_step",
    )(info, mine, other, anchor, momentum, *state)


def shards(
    inputs, output_grads, local_params, first_moment, second_moment, global_params, momentum
):
    n, replicas = lax.axis_size("fsdp"), lax.axis_size("worker")
    me, worker = lax.axis_index("fsdp"), lax.axis_index("worker")
    info = jnp.stack([me, worker % 2, worker]).astype(jnp.int32)
    features = inputs[0]
    rows = local_params.shape[1]
    chunks = chunks_of(rows)
    step = outer_rate * (1.0 + momentum_coef)

    own, parts = split_columns(info, features, n, rows, chunks)
    block, own, parts = lax.optimization_barrier((output_grads[0], own, parts))
    gs, columns, ks = exchange(Mover(), block, own, parts)
    state = []
    for c, (at, size) in enumerate(chunks):
        xs = columns[c]
        send, keep = inner_step(
            info,
            xs,
            gs,
            local_params,
            first_moment,
            second_moment,
            global_params,
            momentum,
            float(replicas),
            at,
            size,
        )
        if c + 1 < len(chunks):
            pinned = [columns[c + 1][k] for k in ks[:PINNED]]
            send, keep, _ = lax.optimization_barrier((send, keep, pinned))
        total = keep + lax.ppermute(send, "worker", pairs(replicas, 1))
        k = 2
        while k < replicas:
            half = total.astype(jnp.float16)
            got = lax.ppermute(half, "worker", pairs(replicas, k))
            if k * 2 >= replicas and c + 1 == len(chunks):
                got, state = lax.optimization_barrier((got, state))
            total = half.astype(jnp.float32) + got.astype(jnp.float32)
            k *= 2
        mine = total * (step / replicas)
        other = lax.ppermute(mine, "worker", pairs(replicas, 1))
        state = outer_step(info, mine, other, global_params, momentum, state, rows, at)
    return tuple(state)


def solution(mesh):
    return jax.shard_map(
        shards,
        mesh=mesh,
        in_specs=(
            P("worker", "fsdp", None),
            P("worker", "fsdp", None),
            P("worker", "fsdp", None),
            P("worker", "fsdp", None),
            P("worker", "fsdp", None),
            P(("fsdp", "worker"), None),
            P(("fsdp", "worker"), None),
        ),
        out_specs=(P("fsdp", None), P(("fsdp", "worker"), None)),
        check_vma=False,
    )
```

```python
import functools
import math

import jax
import jax.numpy as jnp
from jax import lax
from jax.experimental import pallas as pl
from jax.experimental.pallas import tpu as pltpu
from jax.sharding import PartitionSpec as P

beta_first = 0.8
beta_second = 0.9
inner_rate = 0.15
weight_decay = 0.1
adam_epsilon = 1e-08
outer_rate = 0.7
momentum_coef = 0.9
inner_count = 50

TILE = 128
VMEM = 40 * 1024 * 1024
SPLIT_VMEM = 60 * 1024 * 1024


ORDER = ("g2", "y0", "n0", "g1", "x00", "g3", "y1", "x01", "y2", "x03", "n1", "x02", "y3", "n2", "x10", "x11", "x12", "x13")
WINDOW = 5
SIZES = (6, 2)
SENT = (6, 2)
STEP_PINS = (("x10", "x11"),)
CORE_PINS = ((),)
CHIP_PINS = (("x12",),)
BLOCK = 256


def chunks_of(rows, sizes):
    units = rows // TILE
    if sum(sizes) != units:
        sizes = [units - len(sizes) + 1] + [1] * (len(sizes) - 1)
    result, at = [], 0
    for size in sizes:
        result.append((at, size * TILE))
        at += size * TILE
    return result


def pairs(n, k, keep=lambda i: True):
    return [(i, i ^ k) for i in range(n) if keep(i)]


def split_kernel(n, rows, pieces, info, x, *refs):
    outs, (buf, sem_in, sem_out) = refs[:-3], refs[-3:]
    reads, writes = [], []
    for k in range(n):
        start = pl.multiple_of((info[0] ^ k) * rows, TILE)
        reads.append(
            pltpu.make_async_copy(x.at[:, pl.ds(start, rows)], buf.at[k], sem_in.at[k])
        )
        reads[-1].start()
    for k in range(n):
        reads[k].wait()
        for j, (of, at, size) in enumerate(pieces):
            if of == k:
                copy = pltpu.make_async_copy(buf.at[k, :, pl.ds(at, size)], outs[j], sem_out.at[j])
                copy.start()
                writes.append(copy)
    for copy in writes:
        copy.wait()


def split_columns(info, x, n, rows, chunks):
    far = n // 2
    pieces = [(k, 0, rows) for k in range(far)]
    pieces += [(k, at, size) for at, size in chunks for k in range(far, n)]
    shapes = [jax.ShapeDtypeStruct((x.shape[0], size), x.dtype) for _, _, size in pieces]
    flat = pl.pallas_call(
        functools.partial(split_kernel, n, rows, pieces),
        in_specs=[pl.BlockSpec(memory_space=pltpu.SMEM), pl.BlockSpec(memory_space=pltpu.HBM)],
        out_specs=[pl.BlockSpec(memory_space=pltpu.HBM)] * len(shapes),
        scratch_shapes=[
            pltpu.VMEM((n, x.shape[0], rows), x.dtype),
            pltpu.SemaphoreType.DMA((n,)),
            pltpu.SemaphoreType.DMA((len(pieces),)),
        ],
        out_shape=shapes,
        compiler_params=pltpu.CompilerParams(vmem_limit_bytes=SPLIT_VMEM),
        name="split_columns",
    )(info, x)
    return flat[:far], [flat[far * (c + 1) : far * (c + 2)] for c in range(len(chunks))]


def exchange(block, whole, parts):
    n = lax.axis_size("fsdp")
    near, far = n // 4, n // 2
    gs = {0: block}
    xs = [{k: whole[k] for k in range(far)} for _ in parts]
    inside = [range(1, near), [near], range(near + 1, far)]
    crossing = [[far], [far + near], range(far + 1, far + near), range(far + near + 1, n)]
    arrived = {}
    for j, name in enumerate(ORDER):
        kind, which = name[0], int(name[1:])
        if kind == "g":
            jobs = [(which * near, gs[far] if which == 3 else block, near if which == 3 else which * near)]
        elif kind == "y":
            jobs = [(which * near + k, gs[which * near], k) for k in range(1, near)]
        elif kind == "n":
            jobs = [(k, whole[k], k) for k in inside[which]]
        else:
            jobs = [(k, parts[which // 10][k - far], k) for k in crossing[which % 10]]
        after = arrived[ORDER[j - WINDOW]] if j >= WINDOW else []
        if name in ("y1", "g3"):
            after = [after, whole, parts]
        arrived[name] = []
        for key, value, k in jobs:
            if after:
                value, _ = lax.optimization_barrier((value, after))
            moved = lax.ppermute(value, "fsdp", pairs(n, k))
            arrived[name].append(moved)
            if kind in "gy":
                gs[key] = moved
            elif kind == "n":
                for x in xs:
                    x[key] = moved
            else:
                xs[which // 10][key] = moved
    return [gs[k] for k in range(n)], [[x[k] for k in range(n)] for x in xs], arrived


def step_kernel(n, at, share, scale, info, *refs):
    xs, gs = refs[:n], refs[n : 2 * n]
    params, first, second, anchor, momentum, send, keep = refs[2 * n :]
    gradient = None
    for x, g in zip(xs, gs):
        term = lax.dot_general(
            x[...], g[...], (((0,), (0,)), ((), ())), preferred_element_type=jnp.float32
        )
        gradient = term if gradient is None else gradient + term
    moment_one = beta_first * first[0] + (1.0 - beta_first) * gradient
    moment_two = beta_second * second[0] + (1.0 - beta_second) * gradient * gradient
    first_correction = 1.0 - beta_first**inner_count
    second_correction = 1.0 - beta_second**inner_count
    ratio = (
        moment_one
        * (1.0 / first_correction)
        / (jnp.sqrt(moment_two * (1.0 / second_correction)) + adam_epsilon)
    )
    stepped = params[0] - inner_rate * (ratio + weight_decay * params[0])
    core, worker = info[1], info[2]
    half = stepped.shape[1] // 2
    block = stepped.shape[0]
    piece = min(share, block)
    offset = worker * share - (at + pl.program_id(0) * block)
    inside = (offset > -share) & (offset < block)

    def store(left, right):
        left[...] = stepped[:, :half]
        right[...] = stepped[:, half:]

        @pl.when(inside)
        def _():
            rows = pl.ds(pl.multiple_of(jnp.maximum(offset, 0), piece), piece)
            term = owner_term(anchor[...], momentum[...], scale)
            left[rows] += term[:, :half]
            right[rows] += term[:, half:]

    pl.when(core == 0)(lambda: store(keep, send))
    pl.when(core != 0)(lambda: store(send, keep))


def owner_term(anchor, momentum, scale):
    step = outer_rate * (1.0 + momentum_coef)
    return (scale * (1.0 - step) / step) * anchor - (
        scale * outer_rate * momentum_coef**2 / step
    ) * momentum


def inner_step(info, xs, gs, params, first, second, anchor, momentum, scale, at, size):
    n = len(gs)
    tokens, width = gs[0].shape
    share = anchor.shape[0]
    block = math.gcd(size, BLOCK)
    piece = min(share, block)

    def owned(i, info):
        ahead = at + i * block - info[2] * share
        return (jnp.clip(ahead // piece, 0, share // piece - 1), 0)

    columns = [
        pl.BlockSpec(
            (pl.Element(tokens), pl.Element(block)),
            lambda i, info, skip=at - start: (0, pl.multiple_of(skip + i * block, TILE)),
        )
        for _, start in xs
    ]
    whole = pl.BlockSpec((tokens, width), lambda i, info: (0, 0))
    state = pl.BlockSpec((pl.Element(1), pl.Element(block), pl.Element(width)), lambda i, info: (0, pl.multiple_of(at + i * block, TILE), 0))
    part = pl.BlockSpec((block, width // 2), lambda i, info: (i, 0))
    shape = jax.ShapeDtypeStruct((size, width // 2), jnp.float32)
    return pl.pallas_call(
        functools.partial(step_kernel, n, at, share, scale),
        grid_spec=pltpu.PrefetchScalarGridSpec(
            num_scalar_prefetch=1,
            grid=(size // block,),
            in_specs=columns
            + [whole] * n
            + [state] * 3
            + [pl.BlockSpec((piece, width), owned)] * 2,
            out_specs=[part, part],
        ),
        out_shape=[shape, shape],
        compiler_params=pltpu.CompilerParams(vmem_limit_bytes=VMEM),
        name="inner_step",
    )(info, *[x for x, _ in xs], *gs, params, first, second, anchor, momentum)


def outer_kernel(at, share, info, mine, other, anchor, momentum, *refs):
    whole, fresh, buf, sem, sem_fresh = refs[-5:]
    core, worker = info[1], info[2]
    size, half = mine.shape
    copies = []
    for j, (source, side) in enumerate(((mine, core), (other, 1 - core))):
        columns = pl.ds(pl.multiple_of(side * half, half), half)
        copies.append(
            pltpu.make_async_copy(source, whole.at[pl.ds(at, size), columns], sem.at[j])
        )
        copies[-1].start()
    step = outer_rate * (1.0 + momentum_coef)
    piece = min(share, TILE)
    for p in range(share // piece):
        row = worker * share + p * piece - at
        part = pl.ds(p * piece, piece)

        @pl.when((row >= 0) & (row < size))
        def _(row=row, part=part, p=p):
            rows = pl.ds(pl.multiple_of(row, piece), piece)

            def write(left, right):
                base = (momentum_coef - outer_rate * momentum_coef**2 / step) * momentum[part] + (
                    1.0 + (1.0 - step) / step
                ) * anchor[part]
                buf[part, :half] = base[:, :half] - (1.0 / step) * left[rows]
                buf[part, half:] = base[:, half:] - (1.0 / step) * right[rows]

            pl.when(core == 0)(lambda: write(mine, other))
            pl.when(core != 0)(lambda: write(other, mine))
            copy = pltpu.make_async_copy(buf.at[part], fresh.at[part], sem_fresh.at[p])
            copy.start()
            copy.wait()

    for copy in copies:
        copy.wait()


def outer_step(info, mine, other, anchor, momentum, state, rows, at):
    share, width = anchor.shape
    shapes = [
        jax.ShapeDtypeStruct((rows, width), jnp.float32),
        jax.ShapeDtypeStruct((share, width), jnp.float32),
    ]
    return pl.pallas_call(
        functools.partial(outer_kernel, at, share),
        in_specs=[pl.BlockSpec(memory_space=pltpu.SMEM)]
        + [pl.BlockSpec(memory_space=pltpu.VMEM)] * 4
        + [pl.BlockSpec(memory_space=pl.ANY)] * len(state),
        out_specs=[pl.BlockSpec(memory_space=pl.ANY)] * 2,
        out_shape=shapes,
        scratch_shapes=[
            pltpu.VMEM((share, width), jnp.float32),
            pltpu.SemaphoreType.DMA((2,)),
            pltpu.SemaphoreType.DMA((share // min(share, TILE),)),
        ],
        input_output_aliases={5: 0, 6: 1} if state else {},
        compiler_params=pltpu.CompilerParams(vmem_limit_bytes=VMEM),
        name="outer_step",
    )(info, mine, other, anchor, momentum, *state)


def shards(
    inputs, output_grads, local_params, first_moment, second_moment, global_params, momentum
):
    n, replicas = lax.axis_size("fsdp"), lax.axis_size("worker")
    me, worker = lax.axis_index("fsdp"), lax.axis_index("worker")
    info = jnp.stack([me, worker % 2, worker]).astype(jnp.int32)
    features = inputs[0]
    rows = local_params.shape[1]
    chunks = chunks_of(rows, SIZES)
    sent = chunks_of(rows, SENT)
    step = outer_rate * (1.0 + momentum_coef)

    own, parts = split_columns(info, features, n, rows, sent)
    gs, columns, arrived = exchange(output_grads[0], own, parts)
    state, waiting = [], ()
    for c, (at, size) in enumerate(chunks):
        part = max(j for j, (start, _) in enumerate(sent) if start <= at)
        xs = [(x, 0 if k < n // 2 else sent[part][0]) for k, x in enumerate(columns[part])]
        send, keep = inner_step(
            info,
            xs,
            gs,
            local_params,
            first_moment,
            second_moment,
            global_params,
            momentum,
            float(replicas),
            at,
            size,
        )
        pins = [
            [arrived[name] for name in table[c]] if c + 1 < len(chunks) else []
            for table in (STEP_PINS, CORE_PINS, CHIP_PINS)
        ]
        send, keep, _ = lax.optimization_barrier((send, keep, pins[0]))
        got = lax.ppermute(send, "worker", pairs(replicas, 1))
        got, _ = lax.optimization_barrier((got, pins[1]))
        total = keep + got
        k = 2
        while k < replicas:
            half = total.astype(jnp.float16)
            if k == 2 and waiting:
                if state:
                    half, state = lax.optimization_barrier((half, state))
                state = outer_step(info, *waiting, global_params, momentum, state, rows, chunks[c - 1][0])
            got = lax.ppermute(half, "worker", pairs(replicas, k))
            if k == 2:
                got, _ = lax.optimization_barrier((got, pins[2]))
            total = half.astype(jnp.float32) + got.astype(jnp.float32)
            k *= 2
        mine = total * (step / replicas)
        other = lax.ppermute(mine, "worker", pairs(replicas, 1))
        waiting = (mine, other)
    return tuple(outer_step(info, *waiting, global_params, momentum, state, rows, at))


def solution(mesh):
    return jax.shard_map(
        shards,
        mesh=mesh,
        in_specs=(
            P("worker", "fsdp", None),
            P("worker", "fsdp", None),
            P("worker", "fsdp", None),
            P("worker", "fsdp", None),
            P("worker", "fsdp", None),
            P(("fsdp", "worker"), None),
            P(("fsdp", "worker"), None),
        ),
        out_specs=(P("fsdp", None), P(("fsdp", "worker"), None)),
        check_vma=False,
    )
```

```python
import functools
import math

import jax
import jax.numpy as jnp
from jax import lax
from jax.experimental import pallas as pl
from jax.experimental.pallas import tpu as pltpu
from jax.sharding import PartitionSpec as P

beta_first = 0.8
beta_second = 0.9
inner_rate = 0.15
weight_decay = 0.1
adam_epsilon = 1e-08
outer_rate = 0.7
momentum_coef = 0.9
inner_count = 50

TILE = 128
VMEM = 40 * 1024 * 1024
SPLIT_VMEM = 60 * 1024 * 1024


ORDER = ("g2", "x00", "y0", "g1", "g3", "n0", "y1", "x01", "y2", "x03", "n1", "x02", "y3", "n2", "x10", "x12", "x11", "x13")
WINDOW = 5
SIZES = (6, 2)
SENT = (6, 2)
STEP_PINS = (("x10", "x11"),)
CORE_PINS = ((),)
CHIP_PINS = (("x12",),)
BLOCK = 256


def chunks_of(rows, sizes):
    units = rows // TILE
    if sum(sizes) != units:
        sizes = [units - len(sizes) + 1] + [1] * (len(sizes) - 1)
    result, at = [], 0
    for size in sizes:
        result.append((at, size * TILE))
        at += size * TILE
    return result


def pairs(n, k, keep=lambda i: True):
    return [(i, i ^ k) for i in range(n) if keep(i)]


def split_kernel(n, rows, pieces, info, x, *refs):
    outs, (buf, sem_in, sem_out) = refs[:-3], refs[-3:]
    reads, writes = [], []
    for k in range(n):
        start = pl.multiple_of((info[0] ^ k) * rows, TILE)
        reads.append(
            pltpu.make_async_copy(x.at[:, pl.ds(start, rows)], buf.at[k], sem_in.at[k])
        )
        reads[-1].start()
    for k in range(n):
        reads[k].wait()
        for j, (of, at, size) in enumerate(pieces):
            if of == k:
                copy = pltpu.make_async_copy(buf.at[k, :, pl.ds(at, size)], outs[j], sem_out.at[j])
                copy.start()
                writes.append(copy)
    for copy in writes:
        copy.wait()


def split_columns(info, x, n, rows, chunks):
    far = n // 2
    pieces = [(k, 0, rows) for k in range(far)]
    pieces += [(k, at, size) for at, size in chunks for k in range(far, n)]
    shapes = [jax.ShapeDtypeStruct((x.shape[0], size), x.dtype) for _, _, size in pieces]
    flat = pl.pallas_call(
        functools.partial(split_kernel, n, rows, pieces),
        in_specs=[pl.BlockSpec(memory_space=pltpu.SMEM), pl.BlockSpec(memory_space=pltpu.HBM)],
        out_specs=[pl.BlockSpec(memory_space=pltpu.HBM)] * len(shapes),
        scratch_shapes=[
            pltpu.VMEM((n, x.shape[0], rows), x.dtype),
            pltpu.SemaphoreType.DMA((n,)),
            pltpu.SemaphoreType.DMA((len(pieces),)),
        ],
        out_shape=shapes,
        compiler_params=pltpu.CompilerParams(vmem_limit_bytes=SPLIT_VMEM),
        name="split_columns",
    )(info, x)
    return flat[:far], [flat[far * (c + 1) : far * (c + 2)] for c in range(len(chunks))]


def exchange(block, whole, parts):
    n = lax.axis_size("fsdp")
    near, far = n // 4, n // 2
    gs = {0: block}
    xs = [{k: whole[k] for k in range(far)} for _ in parts]
    inside = [range(1, near), [near], range(near + 1, far)]
    crossing = [[far], [far + near], range(far + 1, far + near), range(far + near + 1, n)]
    arrived = {}
    for j, name in enumerate(ORDER):
        kind, which = name[0], int(name[1:])
        if kind == "g":
            jobs = [(which * near, gs[far] if which == 3 else block, near if which == 3 else which * near)]
        elif kind == "y":
            jobs = [(which * near + k, gs[which * near], k) for k in range(1, near)]
        elif kind == "n":
            jobs = [(k, whole[k], k) for k in inside[which]]
        else:
            jobs = [(k, parts[which // 10][k - far], k) for k in crossing[which % 10]]
        after = arrived[ORDER[j - WINDOW]] if j >= WINDOW else []
        if name in ("y1", "g3"):
            after = [after, whole, parts]
        arrived[name] = []
        for key, value, k in jobs:
            if after:
                value, _ = lax.optimization_barrier((value, after))
            moved = lax.ppermute(value, "fsdp", pairs(n, k))
            arrived[name].append(moved)
            if kind in "gy":
                gs[key] = moved
            elif kind == "n":
                for x in xs:
                    x[key] = moved
            else:
                xs[which // 10][key] = moved
    return [gs[k] for k in range(n)], [[x[k] for k in range(n)] for x in xs], arrived


def step_kernel(n, at, share, scale, info, *refs):
    xs, gs = refs[:n], refs[n : 2 * n]
    params, first, second, anchor, momentum, send, keep = refs[2 * n :]
    gradient = None
    for x, g in zip(xs, gs):
        term = lax.dot_general(
            x[...], g[...], (((0,), (0,)), ((), ())), preferred_element_type=jnp.float32
        )
        gradient = term if gradient is None else gradient + term
    moment_one = beta_first * first[0] + (1.0 - beta_first) * gradient
    moment_two = beta_second * second[0] + (1.0 - beta_second) * gradient * gradient
    first_correction = 1.0 - beta_first**inner_count
    second_correction = 1.0 - beta_second**inner_count
    ratio = (
        moment_one
        * (1.0 / first_correction)
        / (jnp.sqrt(moment_two * (1.0 / second_correction)) + adam_epsilon)
    )
    stepped = params[0] - inner_rate * (ratio + weight_decay * params[0])
    core, worker = info[1], info[2]
    half = stepped.shape[1] // 2
    block = stepped.shape[0]
    piece = min(share, block)
    offset = worker * share - (at + pl.program_id(0) * block)
    inside = (offset > -share) & (offset < block)

    def store(left, right):
        left[...] = stepped[:, :half]
        right[...] = stepped[:, half:]

        @pl.when(inside)
        def _():
            rows = pl.ds(pl.multiple_of(jnp.maximum(offset, 0), piece), piece)
            term = owner_term(anchor[...], momentum[...], scale)
            left[rows] += term[:, :half]
            right[rows] += term[:, half:]

    pl.when(core == 0)(lambda: store(keep, send))
    pl.when(core != 0)(lambda: store(send, keep))


def owner_term(anchor, momentum, scale):
    step = outer_rate * (1.0 + momentum_coef)
    return (scale * (1.0 - step) / step) * anchor - (
        scale * outer_rate * momentum_coef**2 / step
    ) * momentum


def inner_step(info, xs, gs, params, first, second, anchor, momentum, scale, at, size):
    n = len(gs)
    tokens, width = gs[0].shape
    share = anchor.shape[0]
    block = math.gcd(size, BLOCK)
    piece = min(share, block)

    def owned(i, info):
        ahead = at + i * block - info[2] * share
        return (jnp.clip(ahead // piece, 0, share // piece - 1), 0)

    columns = [
        pl.BlockSpec(
            (pl.Element(tokens), pl.Element(block)),
            lambda i, info, skip=at - start: (0, pl.multiple_of(skip + i * block, TILE)),
        )
        for _, start in xs
    ]
    whole = pl.BlockSpec((tokens, width), lambda i, info: (0, 0))
    state = pl.BlockSpec((pl.Element(1), pl.Element(block), pl.Element(width)), lambda i, info: (0, pl.multiple_of(at + i * block, TILE), 0))
    part = pl.BlockSpec((block, width // 2), lambda i, info: (i, 0))
    shape = jax.ShapeDtypeStruct((size, width // 2), jnp.float32)
    return pl.pallas_call(
        functools.partial(step_kernel, n, at, share, scale),
        grid_spec=pltpu.PrefetchScalarGridSpec(
            num_scalar_prefetch=1,
            grid=(size // block,),
            in_specs=columns
            + [whole] * n
            + [state] * 3
            + [pl.BlockSpec((piece, width), owned)] * 2,
            out_specs=[part, part],
        ),
        out_shape=[shape, shape],
        compiler_params=pltpu.CompilerParams(vmem_limit_bytes=VMEM),
        name="inner_step",
    )(info, *[x for x, _ in xs], *gs, params, first, second, anchor, momentum)


def outer_kernel(at, share, info, mine, other, anchor, momentum, *refs):
    whole, fresh, buf, sem, sem_fresh = refs[-5:]
    core, worker = info[1], info[2]
    size, half = mine.shape
    copies = []
    for j, (source, side) in enumerate(((mine, core), (other, 1 - core))):
        columns = pl.ds(pl.multiple_of(side * half, half), half)
        copies.append(
            pltpu.make_async_copy(source, whole.at[pl.ds(at, size), columns], sem.at[j])
        )
        copies[-1].start()
    step = outer_rate * (1.0 + momentum_coef)
    piece = min(share, TILE)
    for p in range(share // piece):
        row = worker * share + p * piece - at
        part = pl.ds(p * piece, piece)

        @pl.when((row >= 0) & (row < size))
        def _(row=row, part=part, p=p):
            rows = pl.ds(pl.multiple_of(row, piece), piece)

            def write(left, right):
                base = (momentum_coef - outer_rate * momentum_coef**2 / step) * momentum[part] + (
                    1.0 + (1.0 - step) / step
                ) * anchor[part]
                buf[part, :half] = base[:, :half] - (1.0 / step) * left[rows]
                buf[part, half:] = base[:, half:] - (1.0 / step) * right[rows]

            pl.when(core == 0)(lambda: write(mine, other))
            pl.when(core != 0)(lambda: write(other, mine))
            copy = pltpu.make_async_copy(buf.at[part], fresh.at[part], sem_fresh.at[p])
            copy.start()
            copy.wait()

    for copy in copies:
        copy.wait()


def outer_step(info, mine, other, anchor, momentum, state, rows, at):
    share, width = anchor.shape
    shapes = [
        jax.ShapeDtypeStruct((rows, width), jnp.float32),
        jax.ShapeDtypeStruct((share, width), jnp.float32),
    ]
    return pl.pallas_call(
        functools.partial(outer_kernel, at, share),
        in_specs=[pl.BlockSpec(memory_space=pltpu.SMEM)]
        + [pl.BlockSpec(memory_space=pltpu.VMEM)] * 4
        + [pl.BlockSpec(memory_space=pl.ANY)] * len(state),
        out_specs=[pl.BlockSpec(memory_space=pl.ANY)] * 2,
        out_shape=shapes,
        scratch_shapes=[
            pltpu.VMEM((share, width), jnp.float32),
            pltpu.SemaphoreType.DMA((2,)),
            pltpu.SemaphoreType.DMA((share // min(share, TILE),)),
        ],
        input_output_aliases={5: 0, 6: 1} if state else {},
        compiler_params=pltpu.CompilerParams(vmem_limit_bytes=VMEM),
        name="outer_step",
    )(info, mine, other, anchor, momentum, *state)


def shards(
    inputs, output_grads, local_params, first_moment, second_moment, global_params, momentum
):
    n, replicas = lax.axis_size("fsdp"), lax.axis_size("worker")
    me, worker = lax.axis_index("fsdp"), lax.axis_index("worker")
    info = jnp.stack([me, worker % 2, worker]).astype(jnp.int32)
    features = inputs[0]
    rows = local_params.shape[1]
    chunks = chunks_of(rows, SIZES)
    sent = chunks_of(rows, SENT)
    step = outer_rate * (1.0 + momentum_coef)

    own, parts = split_columns(info, features, n, rows, sent)
    gs, columns, arrived = exchange(output_grads[0], own, parts)
    state, waiting = [], ()
    for c, (at, size) in enumerate(chunks):
        part = max(j for j, (start, _) in enumerate(sent) if start <= at)
        xs = [(x, 0 if k < n // 2 else sent[part][0]) for k, x in enumerate(columns[part])]
        send, keep = inner_step(
            info,
            xs,
            gs,
            local_params,
            first_moment,
            second_moment,
            global_params,
            momentum,
            float(replicas),
            at,
            size,
        )
        pins = [
            [arrived[name] for name in table[c]] if c + 1 < len(chunks) else []
            for table in (STEP_PINS, CORE_PINS, CHIP_PINS)
        ]
        send, keep, _ = lax.optimization_barrier((send, keep, pins[0]))
        got = lax.ppermute(send, "worker", pairs(replicas, 1))
        got, _ = lax.optimization_barrier((got, pins[1]))
        total = keep + got
        k = 2
        while k < replicas:
            half = total.astype(jnp.float16)
            if k == 2 and waiting:
                if state:
                    half, state = lax.optimization_barrier((half, state))
                state = outer_step(info, *waiting, global_params, momentum, state, rows, chunks[c - 1][0])
            got = lax.ppermute(half, "worker", pairs(replicas, k))
            if k == 2:
                got, _ = lax.optimization_barrier((got, pins[2]))
            total = half.astype(jnp.float32) + got.astype(jnp.float32)
            k *= 2
        mine = total * (step / replicas)
        other = lax.ppermute(mine, "worker", pairs(replicas, 1))
        waiting = (mine, other)
    return tuple(outer_step(info, *waiting, global_params, momentum, state, rows, at))


def solution(mesh):
    return jax.shard_map(
        shards,
        mesh=mesh,
        in_specs=(
            P("worker", "fsdp", None),
            P("worker", "fsdp", None),
            P("worker", "fsdp", None),
            P("worker", "fsdp", None),
            P("worker", "fsdp", None),
            P(("fsdp", "worker"), None),
            P(("fsdp", "worker"), None),
        ),
        out_specs=(P("fsdp", None), P(("fsdp", "worker"), None)),
        check_vma=False,
    )
```

```python
import functools
import math

import jax
import jax.numpy as jnp
from jax import lax
from jax.experimental import pallas as pl
from jax.experimental.pallas import tpu as pltpu
from jax.sharding import PartitionSpec as P

beta_first = 0.8
beta_second = 0.9
inner_rate = 0.15
weight_decay = 0.1
adam_epsilon = 1e-08
outer_rate = 0.7
momentum_coef = 0.9
inner_count = 50

TILE = 128
VMEM = 40 * 1024 * 1024
SPLIT_VMEM = 60 * 1024 * 1024


ORDER = ("g2", "x00", "g1", "y0", "g3", "n0", "y1", "x01", "y2", "x03", "n1", "x02", "y3", "n2", "x10", "x12", "x11", "x13")
WINDOW = 5
SIZES = (6, 2)
SENT = (6, 2)
STEP_PINS = (("x10", "x11"),)
CORE_PINS = ((),)
CHIP_PINS = (("x12", "x13"),)
BLOCK = 256


def chunks_of(rows, sizes):
    units = rows // TILE
    if sum(sizes) != units:
        sizes = [units - len(sizes) + 1] + [1] * (len(sizes) - 1)
    result, at = [], 0
    for size in sizes:
        result.append((at, size * TILE))
        at += size * TILE
    return result


def pairs(n, k, keep=lambda i: True):
    return [(i, i ^ k) for i in range(n) if keep(i)]


def split_kernel(n, rows, pieces, info, x, *refs):
    outs, (buf, sem_in, sem_out) = refs[:-3], refs[-3:]
    reads, writes = [], []
    for k in range(n):
        start = pl.multiple_of((info[0] ^ k) * rows, TILE)
        reads.append(
            pltpu.make_async_copy(x.at[:, pl.ds(start, rows)], buf.at[k], sem_in.at[k])
        )
        reads[-1].start()
    for k in range(n):
        reads[k].wait()
        for j, (of, at, size) in enumerate(pieces):
            if of == k:
                copy = pltpu.make_async_copy(buf.at[k, :, pl.ds(at, size)], outs[j], sem_out.at[j])
                copy.start()
                writes.append(copy)
    for copy in writes:
        copy.wait()


def split_columns(info, x, n, rows, chunks):
    far = n // 2
    pieces = [(k, 0, rows) for k in range(far)]
    pieces += [(k, at, size) for at, size in chunks for k in range(far, n)]
    shapes = [jax.ShapeDtypeStruct((x.shape[0], size), x.dtype) for _, _, size in pieces]
    flat = pl.pallas_call(
        functools.partial(split_kernel, n, rows, pieces),
        in_specs=[pl.BlockSpec(memory_space=pltpu.SMEM), pl.BlockSpec(memory_space=pltpu.HBM)],
        out_specs=[pl.BlockSpec(memory_space=pltpu.HBM)] * len(shapes),
        scratch_shapes=[
            pltpu.VMEM((n, x.shape[0], rows), x.dtype),
            pltpu.SemaphoreType.DMA((n,)),
            pltpu.SemaphoreType.DMA((len(pieces),)),
        ],
        out_shape=shapes,
        compiler_params=pltpu.CompilerParams(vmem_limit_bytes=SPLIT_VMEM),
        name="split_columns",
    )(info, x)
    return flat[:far], [flat[far * (c + 1) : far * (c + 2)] for c in range(len(chunks))]


def exchange(block, whole, parts):
    n = lax.axis_size("fsdp")
    near, far = n // 4, n // 2
    gs = {0: block}
    xs = [{k: whole[k] for k in range(far)} for _ in parts]
    inside = [range(1, near), [near], range(near + 1, far)]
    crossing = [[far], [far + near], range(far + 1, far + near), range(far + near + 1, n)]
    arrived = {}
    for j, name in enumerate(ORDER):
        kind, which = name[0], int(name[1:])
        if kind == "g":
            jobs = [(which * near, gs[far] if which == 3 else block, near if which == 3 else which * near)]
        elif kind == "y":
            jobs = [(which * near + k, gs[which * near], k) for k in range(1, near)]
        elif kind == "n":
            jobs = [(k, whole[k], k) for k in inside[which]]
        else:
            jobs = [(k, parts[which // 10][k - far], k) for k in crossing[which % 10]]
        after = arrived[ORDER[j - WINDOW]] if j >= WINDOW else []
        if name in ("y1", "g3"):
            after = [after, whole, parts]
        arrived[name] = []
        for key, value, k in jobs:
            if after:
                value, _ = lax.optimization_barrier((value, after))
            moved = lax.ppermute(value, "fsdp", pairs(n, k))
            arrived[name].append(moved)
            if kind in "gy":
                gs[key] = moved
            elif kind == "n":
                for x in xs:
                    x[key] = moved
            else:
                xs[which // 10][key] = moved
    return [gs[k] for k in range(n)], [[x[k] for k in range(n)] for x in xs], arrived


def step_kernel(n, at, share, scale, info, *refs):
    xs, gs = refs[:n], refs[n : 2 * n]
    params, first, second, anchor, momentum, send, keep = refs[2 * n :]
    gradient = None
    for x, g in zip(xs, gs):
        term = lax.dot_general(
            x[...], g[...], (((0,), (0,)), ((), ())), preferred_element_type=jnp.float32
        )
        gradient = term if gradient is None else gradient + term
    moment_one = beta_first * first[0] + (1.0 - beta_first) * gradient
    moment_two = beta_second * second[0] + (1.0 - beta_second) * gradient * gradient
    first_correction = 1.0 - beta_first**inner_count
    second_correction = 1.0 - beta_second**inner_count
    ratio = (
        moment_one
        * (1.0 / first_correction)
        / (jnp.sqrt(moment_two * (1.0 / second_correction)) + adam_epsilon)
    )
    stepped = params[0] - inner_rate * (ratio + weight_decay * params[0])
    core, worker = info[1], info[2]
    half = stepped.shape[1] // 2
    block = stepped.shape[0]
    piece = min(share, block)
    offset = worker * share - (at + pl.program_id(0) * block)
    inside = (offset > -share) & (offset < block)

    def store(left, right):
        left[...] = stepped[:, :half]
        right[...] = stepped[:, half:]

        @pl.when(inside)
        def _():
            rows = pl.ds(pl.multiple_of(jnp.maximum(offset, 0), piece), piece)
            term = owner_term(anchor[...], momentum[...], scale)
            left[rows] += term[:, :half]
            right[rows] += term[:, half:]

    pl.when(core == 0)(lambda: store(keep, send))
    pl.when(core != 0)(lambda: store(send, keep))


def owner_term(anchor, momentum, scale):
    step = outer_rate * (1.0 + momentum_coef)
    return (scale * (1.0 - step) / step) * anchor - (
        scale * outer_rate * momentum_coef**2 / step
    ) * momentum


def inner_step(info, xs, gs, params, first, second, anchor, momentum, scale, at, size):
    n = len(gs)
    tokens, width = gs[0].shape
    share = anchor.shape[0]
    block = math.gcd(size, BLOCK)
    piece = min(share, block)

    def owned(i, info):
        ahead = at + i * block - info[2] * share
        return (jnp.clip(ahead // piece, 0, share // piece - 1), 0)

    columns = [
        pl.BlockSpec(
            (pl.Element(tokens), pl.Element(block)),
            lambda i, info, skip=at - start: (0, pl.multiple_of(skip + i * block, TILE)),
        )
        for _, start in xs
    ]
    whole = pl.BlockSpec((tokens, width), lambda i, info: (0, 0))
    state = pl.BlockSpec((pl.Element(1), pl.Element(block), pl.Element(width)), lambda i, info: (0, pl.multiple_of(at + i * block, TILE), 0))
    part = pl.BlockSpec((block, width // 2), lambda i, info: (i, 0))
    shape = jax.ShapeDtypeStruct((size, width // 2), jnp.float32)
    return pl.pallas_call(
        functools.partial(step_kernel, n, at, share, scale),
        grid_spec=pltpu.PrefetchScalarGridSpec(
            num_scalar_prefetch=1,
            grid=(size // block,),
            in_specs=columns
            + [whole] * n
            + [state] * 3
            + [pl.BlockSpec((piece, width), owned)] * 2,
            out_specs=[part, part],
        ),
        out_shape=[shape, shape],
        compiler_params=pltpu.CompilerParams(vmem_limit_bytes=VMEM),
        name="inner_step",
    )(info, *[x for x, _ in xs], *gs, params, first, second, anchor, momentum)


def outer_kernel(at, share, info, mine, other, anchor, momentum, *refs):
    whole, fresh, buf, sem, sem_fresh = refs[-5:]
    core, worker = info[1], info[2]
    size, half = mine.shape
    copies = []
    for j, (source, side) in enumerate(((mine, core), (other, 1 - core))):
        columns = pl.ds(pl.multiple_of(side * half, half), half)
        copies.append(
            pltpu.make_async_copy(source, whole.at[pl.ds(at, size), columns], sem.at[j])
        )
        copies[-1].start()
    step = outer_rate * (1.0 + momentum_coef)
    piece = min(share, TILE)
    for p in range(share // piece):
        row = worker * share + p * piece - at
        part = pl.ds(p * piece, piece)

        @pl.when((row >= 0) & (row < size))
        def _(row=row, part=part, p=p):
            rows = pl.ds(pl.multiple_of(row, piece), piece)

            def write(left, right):
                base = (momentum_coef - outer_rate * momentum_coef**2 / step) * momentum[part] + (
                    1.0 + (1.0 - step) / step
                ) * anchor[part]
                buf[part, :half] = base[:, :half] - (1.0 / step) * left[rows]
                buf[part, half:] = base[:, half:] - (1.0 / step) * right[rows]

            pl.when(core == 0)(lambda: write(mine, other))
            pl.when(core != 0)(lambda: write(other, mine))
            copy = pltpu.make_async_copy(buf.at[part], fresh.at[part], sem_fresh.at[p])
            copy.start()
            copy.wait()

    for copy in copies:
        copy.wait()


def outer_step(info, mine, other, anchor, momentum, state, rows, at):
    share, width = anchor.shape
    shapes = [
        jax.ShapeDtypeStruct((rows, width), jnp.float32),
        jax.ShapeDtypeStruct((share, width), jnp.float32),
    ]
    return pl.pallas_call(
        functools.partial(outer_kernel, at, share),
        in_specs=[pl.BlockSpec(memory_space=pltpu.SMEM)]
        + [pl.BlockSpec(memory_space=pltpu.VMEM)] * 4
        + [pl.BlockSpec(memory_space=pl.ANY)] * len(state),
        out_specs=[pl.BlockSpec(memory_space=pl.ANY)] * 2,
        out_shape=shapes,
        scratch_shapes=[
            pltpu.VMEM((share, width), jnp.float32),
            pltpu.SemaphoreType.DMA((2,)),
            pltpu.SemaphoreType.DMA((share // min(share, TILE),)),
        ],
        input_output_aliases={5: 0, 6: 1} if state else {},
        compiler_params=pltpu.CompilerParams(vmem_limit_bytes=VMEM),
        name="outer_step",
    )(info, mine, other, anchor, momentum, *state)


def shards(
    inputs, output_grads, local_params, first_moment, second_moment, global_params, momentum
):
    n, replicas = lax.axis_size("fsdp"), lax.axis_size("worker")
    me, worker = lax.axis_index("fsdp"), lax.axis_index("worker")
    info = jnp.stack([me, worker % 2, worker]).astype(jnp.int32)
    features = inputs[0]
    rows = local_params.shape[1]
    chunks = chunks_of(rows, SIZES)
    sent = chunks_of(rows, SENT)
    step = outer_rate * (1.0 + momentum_coef)

    own, parts = split_columns(info, features, n, rows, sent)
    gs, columns, arrived = exchange(output_grads[0], own, parts)
    state, waiting = [], ()
    for c, (at, size) in enumerate(chunks):
        part = max(j for j, (start, _) in enumerate(sent) if start <= at)
        xs = [(x, 0 if k < n // 2 else sent[part][0]) for k, x in enumerate(columns[part])]
        send, keep = inner_step(
            info,
            xs,
            gs,
            local_params,
            first_moment,
            second_moment,
            global_params,
            momentum,
            float(replicas),
            at,
            size,
        )
        pins = [
            [arrived[name] for name in table[c]] if c + 1 < len(chunks) else []
            for table in (STEP_PINS, CORE_PINS, CHIP_PINS)
        ]
        send, keep, _ = lax.optimization_barrier((send, keep, pins[0]))
        got = lax.ppermute(send, "worker", pairs(replicas, 1))
        got, _ = lax.optimization_barrier((got, pins[1]))
        total = keep + got
        k = 2
        while k < replicas:
            half = total.astype(jnp.float16)
            if k == 2 and waiting:
                if state:
                    half, state = lax.optimization_barrier((half, state))
                state = outer_step(info, *waiting, global_params, momentum, state, rows, chunks[c - 1][0])
            got = lax.ppermute(half, "worker", pairs(replicas, k))
            if k == 2:
                got, _ = lax.optimization_barrier((got, pins[2]))
            total = half.astype(jnp.float32) + got.astype(jnp.float32)
            k *= 2
        mine = total * (step / replicas)
        other = lax.ppermute(mine, "worker", pairs(replicas, 1))
        waiting = (mine, other)
    return tuple(outer_step(info, *waiting, global_params, momentum, state, rows, at))


def solution(mesh):
    return jax.shard_map(
        shards,
        mesh=mesh,
        in_specs=(
            P("worker", "fsdp", None),
            P("worker", "fsdp", None),
            P("worker", "fsdp", None),
            P("worker", "fsdp", None),
            P("worker", "fsdp", None),
            P(("fsdp", "worker"), None),
            P(("fsdp", "worker"), None),
        ),
        out_specs=(P("fsdp", None), P(("fsdp", "worker"), None)),
        check_vma=False,
    )
```

```python
import functools
import math

import jax
import jax.numpy as jnp
from jax import lax
from jax.experimental import pallas as pl
from jax.experimental.pallas import tpu as pltpu
from jax.sharding import PartitionSpec as P

beta_first = 0.8
beta_second = 0.9
inner_rate = 0.15
weight_decay = 0.1
adam_epsilon = 1e-08
outer_rate = 0.7
momentum_coef = 0.9
inner_count = 50

TILE = 128
VMEM = 40 * 1024 * 1024
SPLIT_VMEM = 60 * 1024 * 1024


ORDER = ("g2", "x00", "g1", "y0", "g3", "n0", "y1", "x01", "y2", "x03", "n1", "x02", "y3", "n2", "x10", "x12", "x11", "x13")
WINDOW = 5
SIZES = (6, 2)
SENT = (6, 2)
STEP_PINS = (("x10", "x11"),)
CORE_PINS = ((),)
CHIP_PINS = (("x12", "x13"),)
BLOCK = 256


def chunks_of(rows, sizes):
    units = rows // TILE
    if sum(sizes) != units:
        sizes = [units - len(sizes) + 1] + [1] * (len(sizes) - 1)
    result, at = [], 0
    for size in sizes:
        result.append((at, size * TILE))
        at += size * TILE
    return result


def pairs(n, k, keep=lambda i: True):
    return [(i, i ^ k) for i in range(n) if keep(i)]


def split_kernel(n, rows, pieces, info, x, *refs):
    outs, (buf, sem_in, sem_out) = refs[:-3], refs[-3:]
    reads, writes = [], []
    for k in range(n):
        start = pl.multiple_of((info[0] ^ k) * rows, TILE)
        reads.append(
            pltpu.make_async_copy(x.at[:, pl.ds(start, rows)], buf.at[k], sem_in.at[k])
        )
        reads[-1].start()
    for k in range(n):
        reads[k].wait()
        for j, (of, at, size) in enumerate(pieces):
            if of == k:
                copy = pltpu.make_async_copy(buf.at[k, :, pl.ds(at, size)], outs[j], sem_out.at[j])
                copy.start()
                writes.append(copy)
    for copy in writes:
        copy.wait()


def split_columns(info, x, n, rows, chunks):
    far = n // 2
    pieces = [(k, 0, rows) for k in range(far)]
    pieces += [(k, at, size) for at, size in chunks for k in range(far, n)]
    shapes = [jax.ShapeDtypeStruct((x.shape[0], size), x.dtype) for _, _, size in pieces]
    flat = pl.pallas_call(
        functools.partial(split_kernel, n, rows, pieces),
        in_specs=[pl.BlockSpec(memory_space=pltpu.SMEM), pl.BlockSpec(memory_space=pltpu.HBM)],
        out_specs=[pl.BlockSpec(memory_space=pltpu.HBM)] * len(shapes),
        scratch_shapes=[
            pltpu.VMEM((n, x.shape[0], rows), x.dtype),
            pltpu.SemaphoreType.DMA((n,)),
            pltpu.SemaphoreType.DMA((len(pieces),)),
        ],
        out_shape=shapes,
        compiler_params=pltpu.CompilerParams(vmem_limit_bytes=SPLIT_VMEM),
        name="split_columns",
    )(info, x)
    return flat[:far], [flat[far * (c + 1) : far * (c + 2)] for c in range(len(chunks))]


def exchange(block, whole, parts):
    n = lax.axis_size("fsdp")
    near, far = n // 4, n // 2
    gs = {0: block}
    xs = [{k: whole[k] for k in range(far)} for _ in parts]
    inside = [range(1, near), [near], range(near + 1, far)]
    crossing = [[far], [far + near], range(far + 1, far + near), range(far + near + 1, n)]
    arrived = {}
    for j, name in enumerate(ORDER):
        kind, which = name[0], int(name[1:])
        if kind == "g":
            jobs = [(which * near, gs[far] if which == 3 else block, near if which == 3 else which * near)]
        elif kind == "y":
            jobs = [(which * near + k, gs[which * near], k) for k in range(1, near)]
        elif kind == "n":
            jobs = [(k, whole[k], k) for k in inside[which]]
        else:
            jobs = [(k, parts[which // 10][k - far], k) for k in crossing[which % 10]]
        after = arrived[ORDER[j - WINDOW]] if j >= WINDOW else []
        if name in ("y1", "g3"):
            after = [after, whole, parts]
        arrived[name] = []
        for key, value, k in jobs:
            if after:
                value, _ = lax.optimization_barrier((value, after))
            moved = lax.ppermute(value, "fsdp", pairs(n, k))
            arrived[name].append(moved)
            if kind in "gy":
                gs[key] = moved
            elif kind == "n":
                for x in xs:
                    x[key] = moved
            else:
                xs[which // 10][key] = moved
    return [gs[k] for k in range(n)], [[x[k] for k in range(n)] for x in xs], arrived


def step_kernel(n, at, share, scale, info, *refs):
    xs, gs = refs[:n], refs[n : 2 * n]
    params, first, second, anchor, momentum, send, keep = refs[2 * n :]
    gradient = None
    for x, g in zip(xs, gs):
        term = lax.dot_general(
            x[...], g[...], (((0,), (0,)), ((), ())), preferred_element_type=jnp.float32
        )
        gradient = term if gradient is None else gradient + term
    moment_one = beta_first * first[0] + (1.0 - beta_first) * gradient
    moment_two = beta_second * second[0] + (1.0 - beta_second) * gradient * gradient
    first_correction = 1.0 - beta_first**inner_count
    second_correction = 1.0 - beta_second**inner_count
    ratio = (
        moment_one
        * (1.0 / first_correction)
        / (jnp.sqrt(moment_two * (1.0 / second_correction)) + adam_epsilon)
    )
    stepped = params[0] - inner_rate * (ratio + weight_decay * params[0])
    core, worker = info[1], info[2]
    half = stepped.shape[1] // 2
    block = stepped.shape[0]
    piece = min(share, block)
    offset = worker * share - (at + pl.program_id(0) * block)
    inside = (offset > -share) & (offset < block)

    def store(left, right):
        left[...] = stepped[:, :half]
        right[...] = stepped[:, half:]

        @pl.when(inside)
        def _():
            rows = pl.ds(pl.multiple_of(jnp.maximum(offset, 0), piece), piece)
            term = owner_term(anchor[...], momentum[...], scale)
            left[rows] += term[:, :half]
            right[rows] += term[:, half:]

    pl.when(core == 0)(lambda: store(keep, send))
    pl.when(core != 0)(lambda: store(send, keep))


def owner_term(anchor, momentum, scale):
    step = outer_rate * (1.0 + momentum_coef)
    return (scale * (1.0 - step) / step) * anchor - (
        scale * outer_rate * momentum_coef**2 / step
    ) * momentum


def inner_step(info, xs, gs, params, first, second, anchor, momentum, scale, at, size):
    n = len(gs)
    tokens, width = gs[0].shape
    share = anchor.shape[0]
    block = math.gcd(size, BLOCK) if size > BLOCK else TILE
    piece = min(share, block)

    def owned(i, info):
        ahead = at + i * block - info[2] * share
        return (jnp.clip(ahead // piece, 0, share // piece - 1), 0)

    columns = [
        pl.BlockSpec(
            (pl.Element(tokens), pl.Element(block)),
            lambda i, info, skip=at - start: (0, pl.multiple_of(skip + i * block, TILE)),
        )
        for _, start in xs
    ]
    whole = pl.BlockSpec((tokens, width), lambda i, info: (0, 0))
    state = pl.BlockSpec((pl.Element(1), pl.Element(block), pl.Element(width)), lambda i, info: (0, pl.multiple_of(at + i * block, TILE), 0))
    part = pl.BlockSpec((block, width // 2), lambda i, info: (i, 0))
    shape = jax.ShapeDtypeStruct((size, width // 2), jnp.float32)
    return pl.pallas_call(
        functools.partial(step_kernel, n, at, share, scale),
        grid_spec=pltpu.PrefetchScalarGridSpec(
            num_scalar_prefetch=1,
            grid=(size // block,),
            in_specs=columns
            + [whole] * n
            + [state] * 3
            + [pl.BlockSpec((piece, width), owned)] * 2,
            out_specs=[part, part],
        ),
        out_shape=[shape, shape],
        compiler_params=pltpu.CompilerParams(vmem_limit_bytes=VMEM),
        name="inner_step",
    )(info, *[x for x, _ in xs], *gs, params, first, second, anchor, momentum)


def outer_kernel(at, share, info, mine, other, anchor, momentum, *refs):
    whole, fresh, buf, sem, sem_fresh = refs[-5:]
    core, worker = info[1], info[2]
    size, half = mine.shape
    copies = []
    for j, (source, side) in enumerate(((mine, core), (other, 1 - core))):
        columns = pl.ds(pl.multiple_of(side * half, half), half)
        copies.append(
            pltpu.make_async_copy(source, whole.at[pl.ds(at, size), columns], sem.at[j])
        )
        copies[-1].start()
    step = outer_rate * (1.0 + momentum_coef)
    piece = min(share, TILE)
    for p in range(share // piece):
        row = worker * share + p * piece - at
        part = pl.ds(p * piece, piece)

        @pl.when((row >= 0) & (row < size))
        def _(row=row, part=part, p=p):
            rows = pl.ds(pl.multiple_of(row, piece), piece)

            def write(left, right):
                base = (momentum_coef - outer_rate * momentum_coef**2 / step) * momentum[part] + (
                    1.0 + (1.0 - step) / step
                ) * anchor[part]
                buf[part, :half] = base[:, :half] - (1.0 / step) * left[rows]
                buf[part, half:] = base[:, half:] - (1.0 / step) * right[rows]

            pl.when(core == 0)(lambda: write(mine, other))
            pl.when(core != 0)(lambda: write(other, mine))
            copy = pltpu.make_async_copy(buf.at[part], fresh.at[part], sem_fresh.at[p])
            copy.start()
            copy.wait()

    for copy in copies:
        copy.wait()


def outer_step(info, mine, other, anchor, momentum, state, rows, at):
    share, width = anchor.shape
    shapes = [
        jax.ShapeDtypeStruct((rows, width), jnp.float32),
        jax.ShapeDtypeStruct((share, width), jnp.float32),
    ]
    return pl.pallas_call(
        functools.partial(outer_kernel, at, share),
        in_specs=[pl.BlockSpec(memory_space=pltpu.SMEM)]
        + [pl.BlockSpec(memory_space=pltpu.VMEM)] * 4
        + [pl.BlockSpec(memory_space=pl.ANY)] * len(state),
        out_specs=[pl.BlockSpec(memory_space=pl.ANY)] * 2,
        out_shape=shapes,
        scratch_shapes=[
            pltpu.VMEM((share, width), jnp.float32),
            pltpu.SemaphoreType.DMA((2,)),
            pltpu.SemaphoreType.DMA((share // min(share, TILE),)),
        ],
        input_output_aliases={5: 0, 6: 1} if state else {},
        compiler_params=pltpu.CompilerParams(vmem_limit_bytes=VMEM),
        name="outer_step",
    )(info, mine, other, anchor, momentum, *state)


def shards(
    inputs, output_grads, local_params, first_moment, second_moment, global_params, momentum
):
    n, replicas = lax.axis_size("fsdp"), lax.axis_size("worker")
    me, worker = lax.axis_index("fsdp"), lax.axis_index("worker")
    info = jnp.stack([me, worker % 2, worker]).astype(jnp.int32)
    features = inputs[0]
    rows = local_params.shape[1]
    chunks = chunks_of(rows, SIZES)
    sent = chunks_of(rows, SENT)
    step = outer_rate * (1.0 + momentum_coef)

    own, parts = split_columns(info, features, n, rows, sent)
    gs, columns, arrived = exchange(output_grads[0], own, parts)
    state, waiting = [], ()
    for c, (at, size) in enumerate(chunks):
        part = max(j for j, (start, _) in enumerate(sent) if start <= at)
        xs = [(x, 0 if k < n // 2 else sent[part][0]) for k, x in enumerate(columns[part])]
        send, keep = inner_step(
            info,
            xs,
            gs,
            local_params,
            first_moment,
            second_moment,
            global_params,
            momentum,
            float(replicas),
            at,
            size,
        )
        pins = [
            [arrived[name] for name in table[c]] if c + 1 < len(chunks) else []
            for table in (STEP_PINS, CORE_PINS, CHIP_PINS)
        ]
        send, keep, _ = lax.optimization_barrier((send, keep, pins[0]))
        got = lax.ppermute(send, "worker", pairs(replicas, 1))
        got, _ = lax.optimization_barrier((got, pins[1]))
        total = keep + got
        k = 2
        while k < replicas:
            half = total.astype(jnp.float16)
            if k == 2 and waiting:
                if state:
                    half, state = lax.optimization_barrier((half, state))
                state = outer_step(info, *waiting, global_params, momentum, state, rows, chunks[c - 1][0])
            got = lax.ppermute(half, "worker", pairs(replicas, k))
            if k == 2:
                got, _ = lax.optimization_barrier((got, pins[2]))
            total = half.astype(jnp.float32) + got.astype(jnp.float32)
            k *= 2
        mine = total * (step / replicas)
        other = lax.ppermute(mine, "worker", pairs(replicas, 1))
        waiting = (mine, other)
    return tuple(outer_step(info, *waiting, global_params, momentum, state, rows, at))


def solution(mesh):
    return jax.shard_map(
        shards,
        mesh=mesh,
        in_specs=(
            P("worker", "fsdp", None),
            P("worker", "fsdp", None),
            P("worker", "fsdp", None),
            P("worker", "fsdp", None),
            P("worker", "fsdp", None),
            P(("fsdp", "worker"), None),
            P(("fsdp", "worker"), None),
        ),
        out_specs=(P("fsdp", None), P(("fsdp", "worker"), None)),
        check_vma=False,
    )
```
